32 devices in a mesh: groups: 2 (over x), store: 16 (over z, y, core), tensor: 1.
Axes of the slice: x: 2, y: 2, z: 4, core: 2. Of those that a mesh axis runs over, the one named last changes fastest.
Arguments:
- tokens: bfloat16 [24576, 8192], P(('groups', 'store'), 'tensor'), parts along dimension 0, may hold values from -6 to 6
- base_weight: bfloat16 [8192, 1024], P('tensor'), may hold values from -0.0625 to 0.0625
- shrink_factors: bfloat16 [64, 16, 8192], P(('groups', 'store'), None, 'tensor'), parts along dimension 0, may hold values from -0.0625 to 0.0625
- expand_factors: bfloat16 [64, 16, 1024], P(('groups', 'store')), parts along dimension 0, may hold values from -1.5 to 1.5
- home_rows: int32 [64], P('groups'), parts along dimension 0, may hold values from 0 to 31, as said below
- requests: int32 [32, 8], P(('groups', 'store')), parts along dimension 0, may hold values from 0 to 31, as said below
- block_slot: int32 [32, 48], P(('groups', 'store')), parts along dimension 0, may hold values from 0 to 7, never falling along the last dimension, each value on 1 to 12 neighbouring positions
Outputs:
- projected: bfloat16 [24576, 1024], P(('groups', 'store', 'tensor')), parts along dimension 0
The draws below stay inside these ranges and needn't reach their ends.
There are 2 independent parts, one for each index of `groups`. The reference program is written for one: setup_inputs(seed, part) draws one part's arguments, and reference() takes and returns one part's arrays. A program takes and returns all parts, laid end to end along the dimension named above; an argument that names none is the same for every part. Nothing has to cross between parts.
Inputs may be any that keep to these rules, and one draw needn't show every extreme that they name: A permutation: adapter a is stored in row home_rows[a], on storing device home_rows[a] // 2. `requests`: the 8 adapters of one replica lie on 8 different storing devices; one storing device holds a request of every replica. `block_slot`: never falling along a replica's blocks; every slot owns 1 to 12 consecutive blocks.
All inputs are finite; a program needn't handle non-finite values.
Results may differ from the reference program's by a relative error of at most 0.001.
Values may be sent and summed in bfloat16 or wider, within the bound.
No kernel may reach another device: no remote copies, remote signals or barrier semaphores. Data moves between devices by JAX's collectives and lax.ppermute only.
A program may use at most 128 MiB of HBM per device.

```python
import math
import jax
import jax.numpy as jnp
import numpy as np
from jax import lax

D = 8192
KV = 1024
R = 16
ROWS_REP = 768
ADP_DEV = 2
SLOTS = 8
ADAPTERS = 32
BLOCKS = 48
SEG_MOST = 12
ROWS = 12288
N_STORE = 16


def home_table(key):
    return jax.random.permutation(key, ADAPTERS).astype(jnp.int32)


def draw_home_rows(key, part):
    table = home_table(key)
    return table


def draw_requests(key, part):
    table = home_table(key)
    key = jax.random.fold_in(key, 7)
    key_hot, key_order, key_slots, key_local = jax.random.split(key, 4)
    hottest = jax.random.randint(key_hot, (), 0, N_STORE)
    scores = jax.random.randint(key_order, (N_STORE, N_STORE - 1), 0, 1 << 20) * N_STORE + jnp.arange(N_STORE - 1)[None, :]
    order = jnp.argsort(scores, axis=1).astype(jnp.int32)
    others = (hottest + 1 + order[:, :SLOTS - 1]) % N_STORE
    owners = jnp.concatenate([jnp.full((N_STORE, 1), hottest, jnp.int32), others.astype(jnp.int32)], axis=1)
    slot_scores = jax.random.randint(key_slots, (N_STORE, SLOTS), 0, 1 << 20) * SLOTS + jnp.arange(SLOTS)[None, :]
    slot_order = jnp.argsort(slot_scores, axis=1)
    owners = jnp.take_along_axis(owners, slot_order, axis=1)
    local_rows = jax.random.randint(key_local, (N_STORE, SLOTS), 0, ADP_DEV)
    stored = owners * ADP_DEV + local_rows
    inverse = jnp.argsort(table).astype(jnp.int32)
    return inverse[stored].astype(jnp.int32)


def block_levels(key, dims, shards, low, top_value):
    def one(dim, blocks):
        heights = jax.random.uniform(jax.random.fold_in(jax.random.fold_in(key, 6), dim), (blocks,), jnp.float32, low / len(shards), top_value / len(shards))
        return jnp.repeat(jnp.exp(heights), dims[dim] // blocks).reshape((-1,) + (1,) * (len(dims) - dim - 1))

    gain = one(*shards[0])
    for cut in shards[1:]:
        gain = gain * one(*cut)
    return gain


def length_profile(count, total, limit, skew):
    portions = [(1 << 20) // math.isqrt(rank ** skew) + 1 for rank in range(2, count + 1)]
    surplus, given = total - limit - (count - 1), [1] * (count - 1)
    while surplus > 0:
        free = [i for i in range(count - 1) if given[i] < limit]
        whole, left = sum([portions[i] for i in free]), surplus
        for i in free:
            addition = min(limit - given[i], max(1, left * portions[i] // whole), surplus)
            given[i] = given[i] + addition
            surplus = surplus - addition
    return np.array([limit] + given)


def uneven(rng, amount, total, limit, slope):
    if amount == 2:
        one = jax.random.randint(rng, (), max(1, total - limit), min(limit, total - 1) + 1)
        return jnp.stack([one, total - one])
    lengths = jnp.asarray(length_profile(amount, total, limit, slope), jnp.int32)
    couples = (amount - 1) // 2
    donor, sink = lengths[1:1 + 2 * couples:2], lengths[2:2 + 2 * couples:2]
    margin = jnp.minimum(donor - 1, limit - sink)
    shifted = jax.random.randint(jax.random.fold_in(rng, 1), (couples,), 0, 1 << 20) % (margin + 1)
    lengths = lengths.at[1:1 + 2 * couples:2].set(donor - shifted).at[2:2 + 2 * couples:2].set(sink + shifted)
    return lengths[jax.random.permutation(jax.random.fold_in(rng, 2), amount)]


def normal_values(own_key, extent, spread, most, cuts=(), held_as=jnp.bfloat16):
    loudness = block_levels(own_key, extent, cuts, -0.22, 0.18) if cuts else 1.0
    drawn = jax.random.normal(own_key, extent, jnp.float32) * spread * loudness
    return jnp.minimum(jnp.maximum(drawn, -most), most).astype(held_as)


def setup_inputs(seed: int = 0, part: int = 0) -> dict:
    arg_keys = jax.random.split(jax.random.key(seed), 8)
    part_splits = jax.random.split(jax.random.fold_in(arg_keys[7], part), 8)
    return {
        "tokens": normal_values(part_splits[0], (ROWS, D), 1.0, 6.0, ((0, 16),)),
        "base_weight": normal_values(arg_keys[1], (D, KV), D ** -0.5, 0.0625),
        "shrink_factors": normal_values(part_splits[2], (ADAPTERS, R, D), D ** -0.5, 0.0625, ((0, 16),)),
        "expand_factors": normal_values(part_splits[3], (ADAPTERS, R, KV), R ** -0.5, 1.5, ((0, 16),)),
        "home_rows": draw_home_rows(jax.random.fold_in(jax.random.fold_in(arg_keys[7], part), 71), part),
        "requests": draw_requests(jax.random.fold_in(jax.random.fold_in(arg_keys[7], part), 71), part),
        "block_slot": jax.vmap(lambda own: jnp.searchsorted(jnp.cumsum(uneven(own, SLOTS, BLOCKS, SEG_MOST, 1)), jnp.arange(BLOCKS), side="right"))(jax.random.split(part_splits[6], N_STORE)).reshape((N_STORE, BLOCKS)).astype(jnp.int32),
    }


def reference(tokens, base_weight, shrink_factors, expand_factors, home_rows, requests, block_slot):
    replicas = tokens.reshape(N_STORE, ROWS_REP, D)

    def one_replica(items):
        replica_rows, wanted_ids, slot_list = items
        stored = home_rows[wanted_ids]
        shrink_sel = shrink_factors[stored].reshape(SLOTS * R, D)
        expand_sel = expand_factors[stored].reshape(SLOTS * R, KV).astype(jnp.float32)
        slot_of_row = jnp.repeat(slot_list, 16)
        column_slot = jnp.arange(SLOTS * R) // R
        row_mask = (slot_of_row[:, None] == column_slot[None, :]).astype(jnp.float32)
        shrink = lax.dot_general(replica_rows, shrink_sel, (((1,), (1,)), ((), ())), preferred_element_type=jnp.float32) * row_mask
        base = jnp.dot(replica_rows, base_weight, preferred_element_type=jnp.float32)
        expand = jnp.dot(shrink, expand_sel, precision=lax.Precision.HIGHEST)
        return (base + expand).astype(jnp.bfloat16)

    result = lax.map(one_replica, (replicas, requests, block_slot))
    return result.reshape(N_STORE * ROWS_REP, KV)
```

```python
import functools

import jax
import jax.numpy as jnp
from jax import lax
from jax.experimental import pallas as pl
from jax.experimental.pallas import tpu as pltpu
from jax.sharding import PartitionSpec as P


def general(tokens, base_weight, shrink_factors, expand_factors, home_rows, requests, block_slot):
    slot_count = requests.shape[1]
    rank = shrink_factors.shape[1]
    width = shrink_factors.shape[2]
    rows_here = tokens.shape[0]
    wanted = requests[0]
    adapters = jnp.arange(home_rows.shape[0], dtype=jnp.int32)
    stored = jnp.sum(jnp.where(wanted[:, None] == adapters[None, :], home_rows[None, :], 0), axis=1)
    both = jnp.concatenate([shrink_factors, expand_factors], axis=2)
    everyone = lax.all_gather(both, "store", axis=0, tiled=True)
    picked = jnp.concatenate(
        [lax.dynamic_slice_in_dim(everyone, stored[s], 1, 0) for s in range(slot_count)], axis=0
    ).reshape(slot_count * rank, -1)
    slot_of_row = jnp.broadcast_to(block_slot[0][:, None], (block_slot.shape[1], 16)).reshape(rows_here)
    column_slot = jnp.arange(slot_count * rank, dtype=jnp.int32) // rank
    mask = (slot_of_row[:, None] == column_slot[None, :]).astype(jnp.float32)
    shrink = lax.dot_general(
        tokens, picked[:, :width], (((1,), (1,)), ((), ())), preferred_element_type=jnp.float32
    )
    shrink = lax.psum_scatter(shrink * mask, "tensor", scatter_dimension=0, tiled=True)
    base = lax.psum_scatter(
        jnp.dot(tokens, base_weight, preferred_element_type=jnp.float32),
        "tensor",
        scatter_dimension=0,
        tiled=True,
    )
    expand = jnp.dot(shrink, picked[:, width:].astype(jnp.float32), precision=lax.Precision.HIGHEST)
    return (base + expand).astype(jnp.bfloat16)


def final_kernel(pieces, sel, tokens, mask, *rest):
    bases, bufs, (out, total, table) = rest[:pieces], rest[pieces:-3], rest[-3:]
    step, last = pl.program_id(0), pl.num_programs(0) - 1
    for i, buf in enumerate(bufs):
        table[pl.ds(16 * i, 16), :] = buf[0]

    @pl.when(step == 0)
    def _():
        total[...] = jnp.zeros_like(total)

    @pl.when(step < last)
    def _():
        total[...] += lax.dot_general(
            tokens[...], table[...], (((1,), (1,)), ((), ())), preferred_element_type=jnp.float32
        )

    @pl.when(step == last)
    def _():
        shrink = total[...] * mask[...].astype(jnp.float32)
        high = shrink.astype(jnp.bfloat16)
        low = (shrink - high.astype(jnp.float32)).astype(jnp.bfloat16)
        wide = out.shape[1] // pieces
        for i, base in enumerate(bases):
            cols = pl.ds(wide * i, wide)
            part = jnp.dot(high, table[:, cols], preferred_element_type=jnp.float32)
            part += jnp.dot(low, table[:, cols], preferred_element_type=jnp.float32)
            out[:, cols] = (base[...] + part).astype(out.dtype)


def finish(sel, tokens, mask, bases, bufs, key_width):
    rows, width = tokens.shape
    rank = bufs[0].shape[1]
    assert width % key_width == 0
    steps = width // key_width
    columns = rank * len(bufs)

    def chosen(i, k, sel):
        return (sel[i], 0, k)

    whole = lambda k, sel: (0, 0)
    return pl.pallas_call(
        functools.partial(final_kernel, len(bases)),
        out_shape=jax.ShapeDtypeStruct((rows, key_width), jnp.bfloat16),
        grid_spec=pltpu.PrefetchScalarGridSpec(
            num_scalar_prefetch=1,
            grid=(steps + 1,),
            in_specs=[
                pl.BlockSpec((rows, key_width), lambda k, sel: (0, jnp.minimum(k, steps - 1))),
                pl.BlockSpec((rows, columns), whole),
            ]
            + [pl.BlockSpec(b.shape, whole) for b in bases]
            + [
                pl.BlockSpec((1, rank, key_width), functools.partial(chosen, i))
                for i in range(len(bufs))
            ],
            out_specs=pl.BlockSpec((rows, key_width), whole),
            scratch_shapes=[
                pltpu.VMEM((rows, columns), jnp.float32),
                pltpu.VMEM((columns, key_width), jnp.bfloat16),
            ],
        ),
        compiler_params=pltpu.CompilerParams(
            dimension_semantics=("arbitrary",), vmem_limit_bytes=40 << 20
        ),
        cost_estimate=pl.CostEstimate(
            flops=2 * rows * width * columns, bytes_accessed=2 * rows * width, transcendentals=0
        ),
        name="shrink_expand",
    )(sel, tokens, mask, *bases, *bufs)


def gridded(tokens, base_weight, shrink_factors, expand_factors, home_rows, requests, block_slot):
    held, rank, width = shrink_factors.shape
    key_width = expand_factors.shape[2]
    rows_here = tokens.shape[0]
    me = lax.axis_index("store")
    z, y, c = me // 4, me // 2 % 2, me % 2
    inner = (z == 1) | (z == 2)

    def along_z(moves):
        return [(4 * a + r, 4 * b + r) for a, b in moves for r in range(4)]

    def along_y(levels):
        return [(4 * a + r, 4 * a + (r ^ 2)) for a in levels for r in range(4)]

    cores = [(i, i ^ 1) for i in range(16)]
    pairs = along_z([(0, 1), (1, 0), (2, 3), (3, 2)])
    middle = along_z([(1, 2), (2, 1)])
    outward = along_z([(1, 0), (2, 3)])
    send = lambda a, p: lax.ppermute(a, "store", p)

    own = jnp.concatenate([shrink_factors, expand_factors], axis=2)
    p1 = send(own, pairs)
    y0 = send(own, along_y(range(4)))
    p2 = send(own, middle)
    p4 = send(p2, outward)
    p3 = send(p1, middle)
    y1 = send(p1, along_y(range(4)))
    y2 = send(p2, along_y([1, 2]))
    p5 = send(p3, outward)
    y4 = send(p4, along_y([0, 3]))
    y3 = send(p3, along_y([1, 2]))
    y5 = send(p5, along_y([0, 3]))
    either = lambda a, b: jnp.where(inner, a, b)
    mine = [own, p1, y0, y1, either(p2, p4), either(p3, p5), either(y2, y4), either(y3, y5)]
    theirs = [send(b, cores) for b in mine]

    second = jnp.where(z < 2, 2, 1)
    third = jnp.where(z < 2, 3, 0)
    chip = lambda level, side: 2 * level + side
    chips = jnp.stack(
        [
            chip(z, y), chip(z ^ 1, y), chip(z, y ^ 1), chip(z ^ 1, y ^ 1),
            chip(second, y), chip(third, y), chip(second, y ^ 1), chip(third, y ^ 1),
        ]
    )
    source = jnp.concatenate([2 * chips + c, 2 * chips + 1 - c]).astype(jnp.int32)
    adapters = jnp.arange(home_rows.shape[0], dtype=jnp.int32)
    stored = jnp.sum(
        jnp.where(requests[0][:, None] == adapters[None, :], home_rows[None, :], 0), axis=1
    )
    hit = source[:, None] == (stored // held)[None, :]
    sel = jnp.sum(jnp.where(hit, (stored % held)[None, :], 0), axis=1)
    slots = jnp.arange(requests.shape[1], dtype=jnp.int32)
    column_slot = jnp.max(jnp.where(hit, slots[None, :], -1), axis=1)
    column_slot = jnp.broadcast_to(column_slot[:, None], (source.shape[0], rank)).reshape(-1)
    row_slot = jnp.broadcast_to(block_slot[0][:, None], (block_slot.shape[1], 16)).reshape(rows_here)
    mask = (row_slot[:, None] == column_slot[None, :]).astype(jnp.bfloat16)

    pieces = 4
    wide = key_width // pieces
    bases = [
        jnp.dot(
            tokens, base_weight[:, wide * i : wide * (i + 1)], preferred_element_type=jnp.float32
        )
        for i in range(pieces)
    ]
    return finish(sel, tokens, mask, bases, mine + theirs, key_width)


def solution(mesh):
    placed = (
        P(("groups", "store"), "tensor"),
        P("tensor", None),
        P(("groups", "store"), None, "tensor"),
        P(("groups", "store"), None, None),
        P("groups"),
        P(("groups", "store"), None),
        P(("groups", "store"), None),
    )
    by_grid = mesh.shape["tensor"] == 1 and mesh.shape["store"] == 16
    return jax.shard_map(
        gridded if by_grid else general,
        mesh=mesh,
        in_specs=placed,
        out_specs=P(("groups", "store", "tensor"), None),
        check_vma=False,
    )
```

```python
import functools

import jax
import jax.numpy as jnp
from jax import lax
from jax.experimental import pallas as pl
from jax.experimental.pallas import tpu as pltpu
from jax.sharding import PartitionSpec as P


def general(tokens, base_weight, shrink_factors, expand_factors, home_rows, requests, block_slot):
    slot_count = requests.shape[1]
    rank = shrink_factors.shape[1]
    width = shrink_factors.shape[2]
    rows_here = tokens.shape[0]
    wanted = requests[0]
    adapters = jnp.arange(home_rows.shape[0], dtype=jnp.int32)
    stored = jnp.sum(jnp.where(wanted[:, None] == adapters[None, :], home_rows[None, :], 0), axis=1)
    both = jnp.concatenate([shrink_factors, expand_factors], axis=2)
    everyone = lax.all_gather(both, "store", axis=0, tiled=True)
    picked = jnp.concatenate(
        [lax.dynamic_slice_in_dim(everyone, stored[s], 1, 0) for s in range(slot_count)], axis=0
    ).reshape(slot_count * rank, -1)
    slot_of_row = jnp.broadcast_to(block_slot[0][:, None], (block_slot.shape[1], 16)).reshape(rows_here)
    column_slot = jnp.arange(slot_count * rank, dtype=jnp.int32) // rank
    mask = (slot_of_row[:, None] == column_slot[None, :]).astype(jnp.float32)
    shrink = lax.dot_general(
        tokens, picked[:, :width], (((1,), (1,)), ((), ())), preferred_element_type=jnp.float32
    )
    shrink = lax.psum_scatter(shrink * mask, "tensor", scatter_dimension=0, tiled=True)
    base = lax.psum_scatter(
        jnp.dot(tokens, base_weight, preferred_element_type=jnp.float32),
        "tensor",
        scatter_dimension=0,
        tiled=True,
    )
    expand = jnp.dot(shrink, picked[:, width:].astype(jnp.float32), precision=lax.Precision.HIGHEST)
    return (base + expand).astype(jnp.bfloat16)


def base_kernel(depth, after, tokens, weight, out):
    step = pl.program_id(0)

    @pl.when(step == 0)
    def _():
        out[...] = jnp.zeros_like(out)

    depth_here = weight.shape[0]
    columns = pl.ds(pl.multiple_of(step * depth, 128), depth_here)
    out[...] += jnp.dot(tokens[:, columns], weight[...], preferred_element_type=jnp.float32)


def base_part(after, tokens, weight, part, parts, streamed=False):
    rows, width = tokens.shape
    wide = weight.shape[1] // parts
    steps = 4
    depth = width // steps
    home = pltpu.HBM if streamed else pltpu.VMEM
    tokens = pltpu.with_memory_space_constraint(tokens, home)
    weight = pltpu.with_memory_space_constraint(weight, pltpu.HBM)
    return pl.pallas_call(
        functools.partial(base_kernel, 0 if streamed else depth),
        out_shape=jax.ShapeDtypeStruct((rows, wide), jnp.float32),
        grid=(steps,),
        in_specs=[
            pl.BlockSpec(memory_space=pl.ANY),
            pl.BlockSpec((rows, depth), lambda k: (0, k))
            if streamed
            else pl.BlockSpec(memory_space=pltpu.VMEM),
            pl.BlockSpec((depth, wide), lambda k: (k, part)),
        ],
        out_specs=pl.BlockSpec((rows, wide), lambda k: (0, 0)),
        compiler_params=pltpu.CompilerParams(
            dimension_semantics=("arbitrary",), vmem_limit_bytes=16 << 20
        ),
        cost_estimate=pl.CostEstimate(
            flops=2 * rows * width * wide, bytes_accessed=2 * width * wide, transcendentals=0
        ),
        name=f"base{part}",
    )(after, tokens, weight)


def finish(choice, tokens, mask, bases, batches, given):
    rows, width = tokens.shape
    _, rank, whole = batches[0][0][0].shape
    key_width = whole - width
    count = len(batches) + len(given)
    last = choice.shape[0] - 1
    pieces = len(bases)
    entries = [entry for batch in batches for entry in batch] + given
    arrays, spots = listed(entries)
    owners = [(i, k, len(batch) > 2) for i, batch in enumerate(batches) for k in range(len(batch))]
    owners += [(len(batches) + i, None, False) for i in range(len(given))]
    places = [(i, buf, row, k, levels) for (i, k, levels), (buf, row) in zip(owners, spots)]
    half = whole // 2

    def kernel(choice, tokens, mask, *rest):
        base_refs, bufs = rest[:pieces], rest[pieces:-3]
        out, table, arrived = rest[-3:]

        def copy(i, buf, row, part):
            columns = pl.ds(half * part, half)
            return pltpu.make_async_copy(
                bufs[buf].at[row, :, columns],
                table.at[pl.ds(rank * i, rank), columns],
                arrived.at[part, i],
            )

        for part in range(2):
            for i, buf, row, k, levels in places:
                if k is None:
                    copy(i, buf, row, part).start()
                else:
                    want = choice[i] == k % 2
                    if levels:
                        want = want & (choice[last] == k // 2)
                    pl.when(want)(copy(i, buf, row, part).start)
        total = None
        for part in range(2):
            for i in range(count):
                copy(i, 0, 0, part).wait()
            columns = pl.ds(half * part, min(half, width - half * part))
            term = lax.dot_general(
                tokens[:, columns],
                table[:, columns],
                (((1,), (1,)), ((), ())),
                preferred_element_type=jnp.float32,
            )
            total = term if total is None else total + term
        shrink = total * mask[...].astype(jnp.float32)
        high = shrink.astype(jnp.bfloat16)
        low = (shrink - high.astype(jnp.float32)).astype(jnp.bfloat16)
        wide = key_width // pieces
        for i, base in enumerate(base_refs):
            cols = pl.ds(width + wide * i, wide)
            part = jnp.dot(high, table[:, cols], preferred_element_type=jnp.float32)
            part += jnp.dot(low, table[:, cols], preferred_element_type=jnp.float32)
            out[:, pl.ds(wide * i, wide)] = (base[...] + part).astype(out.dtype)

    vmem = pl.BlockSpec(memory_space=pltpu.VMEM)
    pin = lambda a: pltpu.with_memory_space_constraint(a, pltpu.VMEM)
    return pl.pallas_call(
        kernel,
        out_shape=jax.ShapeDtypeStruct((rows, key_width), jnp.bfloat16),
        in_specs=[pl.BlockSpec(memory_space=pltpu.SMEM)]
        + [vmem] * (2 + pieces)
        + [pl.BlockSpec(memory_space=pl.ANY)] * len(arrays),
        out_specs=vmem,
        scratch_shapes=[
            pltpu.VMEM((rank * count, whole), jnp.bfloat16),
            pltpu.SemaphoreType.DMA((2, count)),
        ],
        compiler_params=pltpu.CompilerParams(vmem_limit_bytes=24 << 20),
        cost_estimate=pl.CostEstimate(
            flops=2 * rows * width * rank * count,
            bytes_accessed=2 * whole * rank * count,
            transcendentals=0,
        ),
        name="shrink_expand",
    )(choice, pin(tokens), pin(mask), *map(pin, bases), *arrays)


def join_kernel(shrink, expand, out):
    width = shrink.shape[2]
    out[:, :, pl.ds(0, width)] = shrink[...]
    out[:, :, pl.ds(width, expand.shape[2])] = expand[...]


def joined(shrink, expand):
    held, rank, width = shrink.shape
    vmem = pl.BlockSpec(memory_space=pltpu.VMEM)
    return pl.pallas_call(
        join_kernel,
        out_shape=jax.ShapeDtypeStruct((held, rank, width + expand.shape[2]), shrink.dtype),
        in_specs=[vmem] * 2,
        out_specs=vmem,
        compiler_params=pltpu.CompilerParams(vmem_limit_bytes=8 << 20),
        name="join",
    )(shrink, expand)


def listed(entries):
    arrays, places = [], []
    for array, row in entries:
        known = [array is other for other in arrays]
        if True not in known:
            arrays.append(array)
            known.append(True)
        places.append((known.index(True), row))
    return arrays, places


def picked(choice, ids, batches):
    arrays, places = listed([entry for i in ids for entry in batches[i]])
    _, rank, whole = arrays[0].shape
    last = choice.shape[0] - 1
    held = 2

    def kernel(choice, *refs):
        out, n = refs[-1], 0
        for place, i in enumerate(ids):
            for k in range(len(batches[i])):
                want = choice[i] == k % held
                if len(batches[i]) > held:
                    want = want & (choice[last] == k // held)
                array, row = places[n]
                n += 1

                @pl.when(want)
                def _(place=place, array=array, row=row):
                    out[place] = refs[array][row]

    vmem = pl.BlockSpec(memory_space=pltpu.VMEM)
    return pl.pallas_call(
        kernel,
        out_shape=jax.ShapeDtypeStruct((len(ids), rank, whole), arrays[0].dtype),
        in_specs=[pl.BlockSpec(memory_space=pltpu.SMEM)] + [vmem] * len(arrays),
        out_specs=vmem,
        compiler_params=pltpu.CompilerParams(vmem_limit_bytes=16 << 20),
        name="pick" + "_".join(map(str, ids)),
    )(choice, *(pltpu.with_memory_space_constraint(a, pltpu.VMEM) for a in arrays))


def gridded(tokens, base_weight, shrink_factors, expand_factors, home_rows, requests, block_slot):
    held, rank, width = shrink_factors.shape
    rows_here = tokens.shape[0]
    me = lax.axis_index("store")
    z, y, c = me // 4, me // 2 % 2, me % 2
    inner = (z == 1) | (z == 2)

    def along_z(moves):
        return [(4 * a + r, 4 * b + r) for a, b in moves for r in range(4)]

    def along_y(levels):
        return [(4 * a + r, 4 * a + (r ^ 2)) for a in levels for r in range(4)]

    cores = [(i, i ^ 1) for i in range(16)]
    pairs = along_z([(0, 1), (1, 0), (2, 3), (3, 2)])
    middle = along_z([(1, 2), (2, 1)])
    outward = along_z([(1, 0), (2, 3)])
    inward = along_z([(0, 1), (3, 2)])
    every, outer_y, inner_y = along_y(range(4)), along_y([0, 3]), along_y([1, 2])
    send = lambda a, p: lax.ppermute(a, "store", p)
    together = lax.optimization_barrier

    own = joined(shrink_factors, expand_factors)
    p1, p2, y0 = send(own, pairs), send(own, middle), send(own, every)

    adapters = jnp.arange(home_rows.shape[0], dtype=jnp.int32)
    stored = jnp.sum(
        jnp.where(requests[0][:, None] == adapters[None, :], home_rows[None, :], 0), axis=1
    )
    stored_other = send(stored, cores)
    second = jnp.where(z < 2, 2, 1)
    third = jnp.where(z < 2, 3, 0)
    chip = lambda level, side: 2 * level + side
    chips = jnp.stack(
        [
            chip(z, y), chip(z ^ 1, y), chip(z, y ^ 1), chip(z ^ 1, y ^ 1),
            chip(second, y), chip(third, y), chip(second, y ^ 1), chip(third, y ^ 1),
        ]
    )
    here = (2 * chips + c).astype(jnp.int32)
    source = jnp.concatenate([here, (2 * chips + 1 - c).astype(jnp.int32)])
    hit = source[:, None] == (stored // held)[None, :]
    slots = jnp.arange(requests.shape[1], dtype=jnp.int32)
    column_slot = jnp.max(jnp.where(hit, slots[None, :], -1), axis=1)
    column_slot = jnp.broadcast_to(column_slot[:, None], (source.shape[0], rank)).reshape(-1)
    row_slot = jnp.broadcast_to(block_slot[0][:, None], (block_slot.shape[1], 16)).reshape(rows_here)
    mask = (row_slot[:, None] == column_slot[None, :]).astype(jnp.bfloat16)

    def second_wanted(rows):
        return jnp.max(
            jnp.where(here[:, None] == (rows // held)[None, :], (rows % held)[None, :], 0), axis=1
        )

    level = inner.astype(jnp.int32)[None]
    take_mine = jnp.concatenate([second_wanted(stored), level])
    take_other = jnp.concatenate([second_wanted(stored_other), level])

    pieces = 2
    after = lambda *a: together((take_mine, *a))[0]
    part = lambda i, order: base_part(order, tokens, base_weight, i, pieces)
    base0 = base_part(take_mine, tokens, base_weight, 0, pieces, streamed=True)
    p1, p2, y0, base0, mask, take_mine, take_other = together(
        (p1, p2, y0, base0, mask, take_mine, take_other)
    )
    p4, p3 = send(p2, outward), send(p1, middle)
    y1a, y1b = send(p1[:1], every), send(p1[1:], outer_y)
    w1 = send(y0[1:], inward)
    y2 = send(p2, inner_y)
    base1 = part(1, after(p1))
    p4, p3, base1 = together((p4, p3, base1))
    p5a, p5b = send(p3[:1], outward), send(p3[1:], outward)
    y4, y3a = send(p4, outer_y), send(p3[:1], inner_y)
    w2 = send(w1, middle)
    y5a = send(p5a, outer_y)
    w3 = send(w2, outward)

    batches = [
        [(own, 0), (own, 1)],
        [(p1, 0), (p1, 1)],
        [(y0, 0), (y0, 1)],
        [(y1a, 0), (y1b, 0), (y1a, 0), (w1, 0)],
        [(p4, 0), (p4, 1), (p2, 0), (p2, 1)],
        [(p5a, 0), (p5b, 0), (p3, 0), (p3, 1)],
        [(y4, 0), (y4, 1), (y2, 0), (y2, 1)],
        [(y5a, 0), (w3, 0), (y3a, 0), (w2, 0)],
    ]
    given = []
    for ids in ((0, 1, 2, 3, 4), (5, 6), (7,)):
        sent = send(picked(take_other, ids, batches), cores)
        given += [(sent, row) for row in range(len(ids))]
    return finish(take_mine, tokens, mask, [base0, base1], batches, given)


def solution(mesh):
    placed = (
        P(("groups", "store"), "tensor"),
        P("tensor", None),
        P(("groups", "store"), None, "tensor"),
        P(("groups", "store"), None, None),
        P("groups"),
        P(("groups", "store"), None),
        P(("groups", "store"), None),
    )
    by_grid = mesh.shape["tensor"] == 1 and mesh.shape["store"] == 16
    return jax.shard_map(
        gridded if by_grid else general,
        mesh=mesh,
        in_specs=placed,
        out_specs=P(("groups", "store", "tensor"), None),
        check_vma=False,
    )
```

```python
import functools

import jax
import jax.numpy as jnp
from jax import lax
from jax.experimental import pallas as pl
from jax.experimental.pallas import tpu as pltpu
from jax.sharding import PartitionSpec as P


def general(tokens, base_weight, shrink_factors, expand_factors, home_rows, requests, block_slot):
    slot_count = requests.shape[1]
    rank = shrink_factors.shape[1]
    width = shrink_factors.shape[2]
    rows_here = tokens.shape[0]
    wanted = requests[0]
    adapters = jnp.arange(home_rows.shape[0], dtype=jnp.int32)
    stored = jnp.sum(jnp.where(wanted[:, None] == adapters[None, :], home_rows[None, :], 0), axis=1)
    both = jnp.concatenate([shrink_factors, expand_factors], axis=2)
    everyone = lax.all_gather(both, "store", axis=0, tiled=True)
    picked = jnp.concatenate(
        [lax.dynamic_slice_in_dim(everyone, stored[s], 1, 0) for s in range(slot_count)], axis=0
    ).reshape(slot_count * rank, -1)
    slot_of_row = jnp.broadcast_to(block_slot[0][:, None], (block_slot.shape[1], 16)).reshape(rows_here)
    column_slot = jnp.arange(slot_count * rank, dtype=jnp.int32) // rank
    mask = (slot_of_row[:, None] == column_slot[None, :]).astype(jnp.float32)
    shrink = lax.dot_general(
        tokens, picked[:, :width], (((1,), (1,)), ((), ())), preferred_element_type=jnp.float32
    )
    shrink = lax.psum_scatter(shrink * mask, "tensor", scatter_dimension=0, tiled=True)
    base = lax.psum_scatter(
        jnp.dot(tokens, base_weight, preferred_element_type=jnp.float32),
        "tensor",
        scatter_dimension=0,
        tiled=True,
    )
    expand = jnp.dot(shrink, picked[:, width:].astype(jnp.float32), precision=lax.Precision.HIGHEST)
    return (base + expand).astype(jnp.bfloat16)


def base_part(tokens, weight, start, wide, after):
    rows, width = tokens.shape
    chunks = 8
    depth = width // chunks

    def kernel(after, tokens, weight, out, kept, held, arrived):
        copies = []
        for k in range(chunks):
            span = pl.ds(depth * k, depth)
            for source, target, kind in (
                (weight.at[span, pl.ds(start, wide)], held.at[span, :], 0),
                (tokens.at[:, span], kept.at[:, span], 1),
            ):
                copies.append(pltpu.make_async_copy(source, target, arrived.at[kind, k]))
        for copy in copies:
            copy.start()
        for k in range(chunks):
            for copy in copies[2 * k : 2 * k + 2]:
                copy.wait()
            span = pl.ds(depth * k, depth)
            term = jnp.dot(kept[:, span], held[span, :], preferred_element_type=jnp.float32)
            if k == 0:
                out[...] = term
            else:
                out[...] += term

    anywhere = pl.BlockSpec(memory_space=pl.ANY)
    return pl.pallas_call(
        kernel,
        out_shape=jax.ShapeDtypeStruct((rows, wide), jnp.float32),
        in_specs=[anywhere] * 3,
        out_specs=pl.BlockSpec(memory_space=pltpu.VMEM),
        scratch_shapes=[
            pltpu.VMEM((rows, width), tokens.dtype),
            pltpu.VMEM((width, wide), weight.dtype),
            pltpu.SemaphoreType.DMA((2, chunks)),
        ],
        compiler_params=pltpu.CompilerParams(vmem_limit_bytes=32 << 20),
        cost_estimate=pl.CostEstimate(
            flops=2 * rows * width * wide, bytes_accessed=2 * width * wide, transcendentals=0
        ),
        name=f"base{start}",
    )(after, *(pltpu.with_memory_space_constraint(a, pltpu.HBM) for a in (tokens, weight)))


def finish(choice, tokens, mask, bases, batches, given):
    rows, width = tokens.shape
    _, rank, whole = batches[0][0][0].shape
    key_width = whole - width
    count = len(batches) + len(given)
    last = choice.shape[0] - 1
    pieces = len(bases)
    entries = [entry for batch in batches for entry in batch] + given
    arrays, spots = listed(entries)
    owners = [(i, k, len(batch) > 2) for i, batch in enumerate(batches) for k in range(len(batch))]
    owners += [(len(batches) + i, None, False) for i in range(len(given))]
    places = [(i, buf, row, k, levels) for (i, k, levels), (buf, row) in zip(owners, spots)]

    def kernel(choice, tokens, mask, *rest):
        base_refs, bufs, (out, table) = rest[:pieces], rest[pieces:-2], rest[-2:]
        for i, buf, row, k, levels in places:
            at = pl.ds(rank * i, rank)
            if k is None:
                table[at, :] = bufs[buf][row]
                continue
            want = choice[i] == k % 2
            if levels:
                want = want & (choice[last] == k // 2)

            @pl.when(want)
            def _(at=at, buf=buf, row=row):
                table[at, :] = bufs[buf][row]

        shrink = lax.dot_general(
            tokens[...],
            table[:, :width],
            (((1,), (1,)), ((), ())),
            preferred_element_type=jnp.float32,
        )
        shrink = shrink * mask[...].astype(jnp.float32)
        high = shrink.astype(jnp.bfloat16)
        low = (shrink - high.astype(jnp.float32)).astype(jnp.bfloat16)
        start = 0
        for base in base_refs:
            wide = base.shape[1]
            cols = pl.ds(width + start, wide)
            part = jnp.dot(high, table[:, cols], preferred_element_type=jnp.float32)
            part += jnp.dot(low, table[:, cols], preferred_element_type=jnp.float32)
            out[:, pl.ds(start, wide)] = (base[...] + part).astype(out.dtype)
            start += wide

    vmem = pl.BlockSpec(memory_space=pltpu.VMEM)
    pin = lambda a: pltpu.with_memory_space_constraint(a, pltpu.VMEM)
    return pl.pallas_call(
        kernel,
        out_shape=jax.ShapeDtypeStruct((rows, key_width), jnp.bfloat16),
        in_specs=[pl.BlockSpec(memory_space=pltpu.SMEM)]
        + [vmem] * (2 + pieces)
        + [vmem] * len(arrays),
        out_specs=vmem,
        scratch_shapes=[
            pltpu.VMEM((rank * count, whole), jnp.bfloat16),
        ],
        compiler_params=pltpu.CompilerParams(vmem_limit_bytes=24 << 20),
        cost_estimate=pl.CostEstimate(
            flops=2 * rows * width * rank * count,
            bytes_accessed=2 * whole * rank * count,
            transcendentals=0,
        ),
        name="shrink_expand",
    )(choice, pin(tokens), pin(mask), *map(pin, bases), *map(pin, arrays))


def join_kernel(shrink, expand, out, arrived):
    width = shrink.shape[2]
    copies = [
        pltpu.make_async_copy(shrink, out.at[:, :, pl.ds(0, width)], arrived.at[0]),
        pltpu.make_async_copy(expand, out.at[:, :, pl.ds(width, expand.shape[2])], arrived.at[1]),
    ]
    for copy in copies:
        copy.start()
    for copy in copies:
        copy.wait()


def joined(shrink, expand):
    held, rank, width = shrink.shape
    pin = lambda a: pltpu.with_memory_space_constraint(a, pltpu.HBM)
    return pl.pallas_call(
        join_kernel,
        out_shape=jax.ShapeDtypeStruct((held, rank, width + expand.shape[2]), shrink.dtype),
        in_specs=[pl.BlockSpec(memory_space=pl.ANY)] * 2,
        out_specs=pl.BlockSpec(memory_space=pltpu.VMEM),
        scratch_shapes=[pltpu.SemaphoreType.DMA((2,))],
        compiler_params=pltpu.CompilerParams(vmem_limit_bytes=8 << 20),
        name="join",
    )(pin(shrink), pin(expand))


def listed(entries):
    arrays, places = [], []
    for array, row in entries:
        known = [array is other for other in arrays]
        if True not in known:
            arrays.append(array)
            known.append(True)
        places.append((known.index(True), row))
    return arrays, places


def picked(choice, ids, batches):
    arrays, places = listed([entry for i in ids for entry in batches[i]])
    _, rank, whole = arrays[0].shape
    last = choice.shape[0] - 1
    held = 2

    def kernel(choice, *refs):
        out, n = refs[-1], 0
        for place, i in enumerate(ids):
            for k in range(len(batches[i])):
                want = choice[i] == k % held
                if len(batches[i]) > held:
                    want = want & (choice[last] == k // held)
                array, row = places[n]
                n += 1

                @pl.when(want)
                def _(place=place, array=array, row=row):
                    out[place] = refs[array][row]

    vmem = pl.BlockSpec(memory_space=pltpu.VMEM)
    return pl.pallas_call(
        kernel,
        out_shape=jax.ShapeDtypeStruct((len(ids), rank, whole), arrays[0].dtype),
        in_specs=[pl.BlockSpec(memory_space=pltpu.SMEM)] + [vmem] * len(arrays),
        out_specs=vmem,
        compiler_params=pltpu.CompilerParams(vmem_limit_bytes=16 << 20),
        name="pick" + "_".join(map(str, ids)),
    )(choice, *(pltpu.with_memory_space_constraint(a, pltpu.VMEM) for a in arrays))


def gridded(tokens, base_weight, shrink_factors, expand_factors, home_rows, requests, block_slot):
    held, rank, width = shrink_factors.shape
    rows_here = tokens.shape[0]
    me = lax.axis_index("store")
    z, y, c = me // 4, me // 2 % 2, me % 2
    inner = (z == 1) | (z == 2)

    def along_z(moves):
        return [(4 * a + r, 4 * b + r) for a, b in moves for r in range(4)]

    def along_y(levels):
        return [(4 * a + r, 4 * a + (r ^ 2)) for a in levels for r in range(4)]

    cores = [(i, i ^ 1) for i in range(16)]
    pairs = along_z([(0, 1), (1, 0), (2, 3), (3, 2)])
    middle = along_z([(1, 2), (2, 1)])
    outward = along_z([(1, 0), (2, 3)])
    every, outer_y = along_y(range(4)), along_y([0, 3])
    send = lambda a, p: lax.ppermute(a, "store", p)
    together = lax.optimization_barrier

    own = joined(shrink_factors, expand_factors)
    p1, y0, p2 = send(own, pairs), send(own, every), send(own, middle)

    wide = expand_factors.shape[2] // 2
    base0 = base_part(tokens, base_weight, 0, wide, requests)
    p1, p2, y0, base0, home_rows, requests, block_slot = together(
        (p1, p2, y0, base0, home_rows, requests, block_slot)
    )
    either = lambda a, b: jnp.where(inner, a, b)
    m1 = send(either(p2, y0), pairs)
    p3 = send(p1, middle)
    n1 = send(either(p2, p1), every)

    adapters = jnp.arange(home_rows.shape[0], dtype=jnp.int32)
    stored = jnp.sum(
        jnp.where(requests[0][:, None] == adapters[None, :], home_rows[None, :], 0), axis=1
    )
    stored_other = send(stored, cores)
    second = jnp.where(z < 2, 2, 1)
    third = jnp.where(z < 2, 3, 0)
    chip = lambda level, side: 2 * level + side
    chips = jnp.stack(
        [
            chip(z, y), chip(z ^ 1, y), chip(z, y ^ 1), chip(z ^ 1, y ^ 1),
            chip(second, y), chip(third, y), chip(second, y ^ 1), chip(third, y ^ 1),
        ]
    )
    here = (2 * chips + c).astype(jnp.int32)
    source = jnp.concatenate([here, (2 * chips + 1 - c).astype(jnp.int32)])
    hit = source[:, None] == (stored // held)[None, :]
    slots = jnp.arange(requests.shape[1], dtype=jnp.int32)
    column_slot = jnp.max(jnp.where(hit, slots[None, :], -1), axis=1)
    column_slot = jnp.broadcast_to(column_slot[:, None], (source.shape[0], rank)).reshape(-1)
    row_slot = jnp.broadcast_to(block_slot[0][:, None], (block_slot.shape[1], 16)).reshape(rows_here)
    mask = (row_slot[:, None] == column_slot[None, :]).astype(jnp.bfloat16)

    def second_wanted(rows):
        return jnp.max(
            jnp.where(here[:, None] == (rows // held)[None, :], (rows % held)[None, :], 0), axis=1
        )

    level = inner.astype(jnp.int32)[None]
    take_mine = jnp.concatenate([second_wanted(stored), level])
    take_other = jnp.concatenate([second_wanted(stored_other), level])

    after = lambda a: together((requests, a))[0]
    base1 = base_part(tokens, base_weight, wide, wide, after(p1))
    m1, p3, n1, base1, mask, take_mine, take_other = together(
        (m1, p3, n1, base1, mask, take_mine, take_other)
    )
    p5a, n2b = send(p3[:1], outward), send(either(p3, m1)[1:], every)
    p5b, n2a = send(p3[1:], outward), send(either(p3, m1)[:1], every)
    y5, w5 = send(p5a, outer_y), send(n2b, outward)

    batches = [
        [(own, 0), (own, 1)],
        [(p1, 0), (p1, 1)],
        [(y0, 0), (y0, 1)],
        [(n1, 0), (n1, 1), (m1, 0), (m1, 1)],
        [(m1, 0), (m1, 1), (p2, 0), (p2, 1)],
        [(p5a, 0), (p5b, 0), (p3, 0), (p3, 1)],
        [(n2a, 0), (n2b, 0), (n1, 0), (n1, 1)],
        [(y5, 0), (w5, 0), (n2a, 0), (n2b, 0)],
    ]
    given = []
    for ids in ((0, 1, 2, 3, 4), (5, 6), (7,)):
        sent = send(picked(take_other, ids, batches), cores)
        given += [(sent, row) for row in range(len(ids))]
    return finish(take_mine, tokens, mask, [base0, base1], batches, given)


def solution(mesh):
    placed = (
        P(("groups", "store"), "tensor"),
        P("tensor", None),
        P(("groups", "store"), None, "tensor"),
        P(("groups", "store"), None, None),
        P("groups"),
        P(("groups", "store"), None),
        P(("groups", "store"), None),
    )
    by_grid = mesh.shape["tensor"] == 1 and mesh.shape["store"] == 16
    return jax.shard_map(
        gridded if by_grid else general,
        mesh=mesh,
        in_specs=placed,
        out_specs=P(("groups", "store", "tensor"), None),
        check_vma=False,
    )
```

```python
import functools

import jax
import jax.numpy as jnp
from jax import lax
from jax.experimental import pallas as pl
from jax.experimental.pallas import tpu as pltpu
from jax.sharding import PartitionSpec as P


def general(tokens, base_weight, shrink_factors, expand_factors, home_rows, requests, block_slot):
    slot_count = requests.shape[1]
    rank = shrink_factors.shape[1]
    width = shrink_factors.shape[2]
    rows_here = tokens.shape[0]
    wanted = requests[0]
    adapters = jnp.arange(home_rows.shape[0], dtype=jnp.int32)
    stored = jnp.sum(jnp.where(wanted[:, None] == adapters[None, :], home_rows[None, :], 0), axis=1)
    both = jnp.concatenate([shrink_factors, expand_factors], axis=2)
    everyone = lax.all_gather(both, "store", axis=0, tiled=True)
    picked = jnp.concatenate(
        [lax.dynamic_slice_in_dim(everyone, stored[s], 1, 0) for s in range(slot_count)], axis=0
    ).reshape(slot_count * rank, -1)
    slot_of_row = jnp.broadcast_to(block_slot[0][:, None], (block_slot.shape[1], 16)).reshape(rows_here)
    column_slot = jnp.arange(slot_count * rank, dtype=jnp.int32) // rank
    mask = (slot_of_row[:, None] == column_slot[None, :]).astype(jnp.float32)
    shrink = lax.dot_general(
        tokens, picked[:, :width], (((1,), (1,)), ((), ())), preferred_element_type=jnp.float32
    )
    shrink = lax.psum_scatter(shrink * mask, "tensor", scatter_dimension=0, tiled=True)
    base = lax.psum_scatter(
        jnp.dot(tokens, base_weight, preferred_element_type=jnp.float32),
        "tensor",
        scatter_dimension=0,
        tiled=True,
    )
    expand = jnp.dot(shrink, picked[:, width:].astype(jnp.float32), precision=lax.Precision.HIGHEST)
    return (base + expand).astype(jnp.bfloat16)


def base_part(tokens, weight, start, wide, after):
    rows, width = tokens.shape
    chunks = 8
    depth = width // chunks

    def kernel(after, tokens, weight, out, kept, held, arrived):
        copies = []
        for k in range(chunks):
            span = pl.ds(depth * k, depth)
            for source, target, kind in (
                (weight.at[span, pl.ds(start, wide)], held.at[span, :], 0),
                (tokens.at[:, span], kept.at[:, span], 1),
            ):
                copies.append(pltpu.make_async_copy(source, target, arrived.at[kind, k]))
        for copy in copies:
            copy.start()
        for k in range(chunks):
            for copy in copies[2 * k : 2 * k + 2]:
                copy.wait()
            span = pl.ds(depth * k, depth)
            term = jnp.dot(kept[:, span], held[span, :], preferred_element_type=jnp.float32)
            if k == 0:
                out[...] = term
            else:
                out[...] += term

    anywhere = pl.BlockSpec(memory_space=pl.ANY)
    return pl.pallas_call(
        kernel,
        out_shape=jax.ShapeDtypeStruct((rows, wide), jnp.float32),
        in_specs=[anywhere] * 3,
        out_specs=pl.BlockSpec(memory_space=pltpu.VMEM),
        scratch_shapes=[
            pltpu.VMEM((rows, width), tokens.dtype),
            pltpu.VMEM((width, wide), weight.dtype),
            pltpu.SemaphoreType.DMA((2, chunks)),
        ],
        compiler_params=pltpu.CompilerParams(vmem_limit_bytes=32 << 20),
        cost_estimate=pl.CostEstimate(
            flops=2 * rows * width * wide, bytes_accessed=2 * width * wide, transcendentals=0
        ),
        name=f"base{start}",
    )(after, *(pltpu.with_memory_space_constraint(a, pltpu.HBM) for a in (tokens, weight)))


def finish(choice, tokens, mask, bases, batches, given):
    rows, width = tokens.shape
    _, rank, whole = batches[0][0][0].shape
    key_width = whole - width
    count = len(batches) + len(given)
    last = choice.shape[0] - 1
    pieces = len(bases)
    entries = [entry for batch in batches for entry in batch] + given
    arrays, spots = listed(entries)
    owners = [(i, k, len(batch) > 2) for i, batch in enumerate(batches) for k in range(len(batch))]
    owners += [(len(batches) + i, None, False) for i in range(len(given))]
    places = [(i, buf, row, k, levels) for (i, k, levels), (buf, row) in zip(owners, spots)]

    def kernel(choice, tokens, mask, *rest):
        base_refs, bufs, (out, table) = rest[:pieces], rest[pieces:-2], rest[-2:]
        for i, buf, row, k, levels in places:
            at = pl.ds(rank * i, rank)
            if k is None:
                table[at, :] = bufs[buf][row]
                continue
            want = choice[i] == k % 2
            if levels:
                want = want & (choice[last] == k // 2)

            @pl.when(want)
            def _(at=at, buf=buf, row=row):
                table[at, :] = bufs[buf][row]

        shrink = lax.dot_general(
            tokens[...],
            table[:, :width],
            (((1,), (1,)), ((), ())),
            preferred_element_type=jnp.float32,
        )
        shrink = shrink * mask[...].astype(jnp.float32)
        high = shrink.astype(jnp.bfloat16)
        low = (shrink - high.astype(jnp.float32)).astype(jnp.bfloat16)
        start = 0
        for base in base_refs:
            wide = base.shape[1]
            cols = pl.ds(width + start, wide)
            part = jnp.dot(high, table[:, cols], preferred_element_type=jnp.float32)
            part += jnp.dot(low, table[:, cols], preferred_element_type=jnp.float32)
            out[:, pl.ds(start, wide)] = (base[...] + part).astype(out.dtype)
            start += wide

    vmem = pl.BlockSpec(memory_space=pltpu.VMEM)
    pin = lambda a: pltpu.with_memory_space_constraint(a, pltpu.VMEM)
    return pl.pallas_call(
        kernel,
        out_shape=jax.ShapeDtypeStruct((rows, key_width), jnp.bfloat16),
        in_specs=[pl.BlockSpec(memory_space=pltpu.SMEM)]
        + [vmem] * (2 + pieces)
        + [vmem] * len(arrays),
        out_specs=vmem,
        scratch_shapes=[
            pltpu.VMEM((rank * count, whole), jnp.bfloat16),
        ],
        compiler_params=pltpu.CompilerParams(vmem_limit_bytes=24 << 20),
        cost_estimate=pl.CostEstimate(
            flops=2 * rows * width * rank * count,
            bytes_accessed=2 * whole * rank * count,
            transcendentals=0,
        ),
        name="shrink_expand",
    )(choice, pin(tokens), pin(mask), *map(pin, bases), *map(pin, arrays))


def join_kernel(shrink, expand, out, arrived):
    width = shrink.shape[2]
    copies = [
        pltpu.make_async_copy(shrink, out.at[:, :, pl.ds(0, width)], arrived.at[0]),
        pltpu.make_async_copy(expand, out.at[:, :, pl.ds(width, expand.shape[2])], arrived.at[1]),
    ]
    for copy in copies:
        copy.start()
    for copy in copies:
        copy.wait()


def joined(shrink, expand):
    held, rank, width = shrink.shape
    pin = lambda a: pltpu.with_memory_space_constraint(a, pltpu.HBM)
    return pl.pallas_call(
        join_kernel,
        out_shape=jax.ShapeDtypeStruct((held, rank, width + expand.shape[2]), shrink.dtype),
        in_specs=[pl.BlockSpec(memory_space=pl.ANY)] * 2,
        out_specs=pl.BlockSpec(memory_space=pltpu.VMEM),
        scratch_shapes=[pltpu.SemaphoreType.DMA((2,))],
        compiler_params=pltpu.CompilerParams(vmem_limit_bytes=8 << 20),
        name="join",
    )(pin(shrink), pin(expand))


def listed(entries):
    arrays, places = [], []
    for array, row in entries:
        known = [array is other for other in arrays]
        if True not in known:
            arrays.append(array)
            known.append(True)
        places.append((known.index(True), row))
    return arrays, places


def picked(choice, ids, batches):
    arrays, places = listed([entry for i in ids for entry in batches[i]])
    _, rank, whole = arrays[0].shape
    last = choice.shape[0] - 1
    held = 2

    def kernel(choice, *refs):
        out, n = refs[-1], 0
        for place, i in enumerate(ids):
            for k in range(len(batches[i])):
                want = choice[i] == k % held
                if len(batches[i]) > held:
                    want = want & (choice[last] == k // held)
                array, row = places[n]
                n += 1

                @pl.when(want)
                def _(place=place, array=array, row=row):
                    out[place] = refs[array][row]

    vmem = pl.BlockSpec(memory_space=pltpu.VMEM)
    return pl.pallas_call(
        kernel,
        out_shape=jax.ShapeDtypeStruct((len(ids), rank, whole), arrays[0].dtype),
        in_specs=[pl.BlockSpec(memory_space=pltpu.SMEM)] + [vmem] * len(arrays),
        out_specs=vmem,
        compiler_params=pltpu.CompilerParams(vmem_limit_bytes=16 << 20),
        name="pick" + "_".join(map(str, ids)),
    )(choice, *(pltpu.with_memory_space_constraint(a, pltpu.VMEM) for a in arrays))


def gridded(tokens, base_weight, shrink_factors, expand_factors, home_rows, requests, block_slot):
    held, rank, width = shrink_factors.shape
    rows_here = tokens.shape[0]
    me = lax.axis_index("store")
    z, y, c = me // 4, me // 2 % 2, me % 2
    inner = (z == 1) | (z == 2)

    def along_z(moves):
        return [(4 * a + r, 4 * b + r) for a, b in moves for r in range(4)]

    def along_y(levels):
        return [(4 * a + r, 4 * a + (r ^ 2)) for a in levels for r in range(4)]

    cores = [(i, i ^ 1) for i in range(16)]
    pairs = along_z([(0, 1), (1, 0), (2, 3), (3, 2)])
    middle = along_z([(1, 2), (2, 1)])
    outward = along_z([(1, 0), (2, 3)])
    every, outer_y = along_y(range(4)), along_y([0, 3])
    send = lambda a, p: lax.ppermute(a, "store", p)
    together = lax.optimization_barrier

    own = joined(shrink_factors, expand_factors)
    p1, y0, p2 = send(own, pairs), send(own, every), send(own, middle)

    wide = expand_factors.shape[2] // 2
    base0 = base_part(tokens, base_weight, 0, wide, requests)
    p1, p2, y0, base0, home_rows, requests, block_slot = together(
        (p1, p2, y0, base0, home_rows, requests, block_slot)
    )
    either = lambda a, b: jnp.where(inner, a, b)
    for_m1, for_n1, for_p3 = together((either(p2, y0), either(p2, p1), p1))
    m1, n1, p3 = send(for_m1, pairs), send(for_n1, every), send(for_p3, middle)

    adapters = jnp.arange(home_rows.shape[0], dtype=jnp.int32)
    stored = jnp.sum(
        jnp.where(requests[0][:, None] == adapters[None, :], home_rows[None, :], 0), axis=1
    )
    stored_other = send(stored, cores)
    second = jnp.where(z < 2, 2, 1)
    third = jnp.where(z < 2, 3, 0)
    chip = lambda level, side: 2 * level + side
    chips = jnp.stack(
        [
            chip(z, y), chip(z ^ 1, y), chip(z, y ^ 1), chip(z ^ 1, y ^ 1),
            chip(second, y), chip(third, y), chip(second, y ^ 1), chip(third, y ^ 1),
        ]
    )
    here = (2 * chips + c).astype(jnp.int32)
    source = jnp.concatenate([here, (2 * chips + 1 - c).astype(jnp.int32)])
    hit = source[:, None] == (stored // held)[None, :]
    slots = jnp.arange(requests.shape[1], dtype=jnp.int32)
    column_slot = jnp.max(jnp.where(hit, slots[None, :], -1), axis=1)
    column_slot = jnp.broadcast_to(column_slot[:, None], (source.shape[0], rank)).reshape(-1)
    row_slot = jnp.broadcast_to(block_slot[0][:, None], (block_slot.shape[1], 16)).reshape(rows_here)
    mask = (row_slot[:, None] == column_slot[None, :]).astype(jnp.bfloat16)

    def second_wanted(rows):
        return jnp.max(
            jnp.where(here[:, None] == (rows // held)[None, :], (rows % held)[None, :], 0), axis=1
        )

    level = inner.astype(jnp.int32)[None]
    take_mine = jnp.concatenate([second_wanted(stored), level])
    take_other = jnp.concatenate([second_wanted(stored_other), level])

    after = lambda a: together((requests, a))[0]
    base1 = base_part(tokens, base_weight, wide, wide, after(p1))
    m1, n1, p3, base1, mask, take_mine, take_other = together(
        (m1, n1, p3, base1, mask, take_mine, take_other)
    )
    batches = [
        [(own, 0), (own, 1)],
        [(p1, 0), (p1, 1)],
        [(y0, 0), (y0, 1)],
        [(n1, 0), (n1, 1), (m1, 0), (m1, 1)],
        [(m1, 0), (m1, 1), (p2, 0), (p2, 1)],
    ]
    p5a, p5b = send(p3[:1], outward), send(p3[1:], outward)
    for_n2, first = together((either(p3, m1), picked(take_other, range(5), batches)))
    n2b, n2a = send(for_n2[1:], every), send(for_n2[:1], every)
    y5, w5 = send(p5a, outer_y), send(n2b, outward)
    batches += [
        [(p5a, 0), (p5b, 0), (p3, 0), (p3, 1)],
        [(n2a, 0), (n2b, 0), (n1, 0), (n1, 1)],
        [(y5, 0), (w5, 0), (n2a, 0), (n2b, 0)],
    ]
    picks = [first] + [picked(take_other, ids, batches) for ids in ((5, 6), (7,))]
    sent = [send(a, cores) for a in picks]
    given = [(a, row) for a in sent for row in range(a.shape[0])]
    return finish(take_mine, tokens, mask, [base0, base1], batches, given)


def solution(mesh):
    placed = (
        P(("groups", "store"), "tensor"),
        P("tensor", None),
        P(("groups", "store"), None, "tensor"),
        P(("groups", "store"), None, None),
        P("groups"),
        P(("groups", "store"), None),
        P(("groups", "store"), None),
    )
    by_grid = mesh.shape["tensor"] == 1 and mesh.shape["store"] == 16
    return jax.shard_map(
        gridded if by_grid else general,
        mesh=mesh,
        in_specs=placed,
        out_specs=P(("groups", "store", "tensor"), None),
        check_vma=False,
    )
```

```python
import functools

import jax
import jax.numpy as jnp
from jax import lax
from jax.experimental import pallas as pl
from jax.experimental.pallas import tpu as pltpu
from jax.sharding import PartitionSpec as P


def general(tokens, base_weight, shrink_factors, expand_factors, home_rows, requests, block_slot):
    slot_count = requests.shape[1]
    rank = shrink_factors.shape[1]
    width = shrink_factors.shape[2]
    rows_here = tokens.shape[0]
    wanted = requests[0]
    adapters = jnp.arange(home_rows.shape[0], dtype=jnp.int32)
    stored = jnp.sum(jnp.where(wanted[:, None] == adapters[None, :], home_rows[None, :], 0), axis=1)
    both = jnp.concatenate([shrink_factors, expand_factors], axis=2)
    everyone = lax.all_gather(both, "store", axis=0, tiled=True)
    picked = jnp.concatenate(
        [lax.dynamic_slice_in_dim(everyone, stored[s], 1, 0) for s in range(slot_count)], axis=0
    ).reshape(slot_count * rank, -1)
    slot_of_row = jnp.broadcast_to(block_slot[0][:, None], (block_slot.shape[1], 16)).reshape(rows_here)
    column_slot = jnp.arange(slot_count * rank, dtype=jnp.int32) // rank
    mask = (slot_of_row[:, None] == column_slot[None, :]).astype(jnp.float32)
    shrink = lax.dot_general(
        tokens, picked[:, :width], (((1,), (1,)), ((), ())), preferred_element_type=jnp.float32
    )
    shrink = lax.psum_scatter(shrink * mask, "tensor", scatter_dimension=0, tiled=True)
    base = lax.psum_scatter(
        jnp.dot(tokens, base_weight, preferred_element_type=jnp.float32),
        "tensor",
        scatter_dimension=0,
        tiled=True,
    )
    expand = jnp.dot(shrink, picked[:, width:].astype(jnp.float32), precision=lax.Precision.HIGHEST)
    return (base + expand).astype(jnp.bfloat16)


def base_part(tokens, weight, start, wide, after):
    rows, width = tokens.shape
    chunks = 8
    depth = width // chunks

    def kernel(after, tokens, weight, out, kept, held, arrived):
        copies = []
        for k in range(chunks):
            span = pl.ds(depth * k, depth)
            for source, target, kind in (
                (weight.at[span, pl.ds(start, wide)], held.at[span, :], 0),
                (tokens.at[:, span], kept.at[:, span], 1),
            ):
                copies.append(pltpu.make_async_copy(source, target, arrived.at[kind, k]))
        for copy in copies:
            copy.start()
        for k in range(chunks):
            for copy in copies[2 * k : 2 * k + 2]:
                copy.wait()
            span = pl.ds(depth * k, depth)
            term = jnp.dot(kept[:, span], held[span, :], preferred_element_type=jnp.float32)
            if k == 0:
                out[...] = term
            else:
                out[...] += term

    anywhere = pl.BlockSpec(memory_space=pl.ANY)
    return pl.pallas_call(
        kernel,
        out_shape=jax.ShapeDtypeStruct((rows, wide), jnp.float32),
        in_specs=[anywhere] * 3,
        out_specs=pl.BlockSpec(memory_space=pltpu.VMEM),
        scratch_shapes=[
            pltpu.VMEM((rows, width), tokens.dtype),
            pltpu.VMEM((width, wide), weight.dtype),
            pltpu.SemaphoreType.DMA((2, chunks)),
        ],
        compiler_params=pltpu.CompilerParams(vmem_limit_bytes=32 << 20),
        cost_estimate=pl.CostEstimate(
            flops=2 * rows * width * wide, bytes_accessed=2 * width * wide, transcendentals=0
        ),
        name=f"base{start}",
    )(after, *(pltpu.with_memory_space_constraint(a, pltpu.HBM) for a in (tokens, weight)))


def finish(choice, tokens, mask, bases, batches, given):
    rows, width = tokens.shape
    _, rank, whole = batches[0][0][0].shape
    key_width = whole - width
    count = len(batches) + len(given)
    last = choice.shape[0] - 1
    pieces = len(bases)
    entries = [entry for batch in batches for entry in batch] + given
    arrays, spots = listed(entries)
    parts = 2 * pieces
    wide = key_width // parts
    owners = [(i, k, len(batch) > 2) for i, batch in enumerate(batches) for k in range(len(batch))]
    owners += [(len(batches) + i, None, False) for i in range(len(given))]
    places = [(i, buf, row, k, levels) for (i, k, levels), (buf, row) in zip(owners, spots)]

    def kernel(choice, tokens, mask, *rest):
        base_refs, bufs = rest[:pieces], rest[pieces:-4]
        out, table, done, left = rest[-4:]
        for i, buf, row, k, levels in places:
            at = pl.ds(rank * i, rank)
            if k is None:
                table[at, :] = bufs[buf][row]
                continue
            want = choice[i] == k % 2
            if levels:
                want = want & (choice[last] == k // 2)

            @pl.when(want)
            def _(at=at, buf=buf, row=row):
                table[at, :] = bufs[buf][row]

        shrink = lax.dot_general(
            tokens[...],
            table[:, :width],
            (((1,), (1,)), ((), ())),
            preferred_element_type=jnp.float32,
        )
        shrink = shrink * mask[...].astype(jnp.float32)
        high = shrink.astype(jnp.bfloat16)
        low = (shrink - high.astype(jnp.float32)).astype(jnp.bfloat16)
        copies = []
        for i in range(parts):
            start = wide * i
            each = parts // pieces
            base = base_refs[i // each][:, pl.ds(wide * (i % each), wide)]
            cols = pl.ds(width + start, wide)
            part = jnp.dot(high, table[:, cols], preferred_element_type=jnp.float32)
            part += jnp.dot(low, table[:, cols], preferred_element_type=jnp.float32)
            done[i] = (base + part).astype(out.dtype)
            copies.append(
                pltpu.make_async_copy(done.at[i], out.at[:, pl.ds(start, wide)], left.at[i])
            )
            copies[-1].start()
        for copy in copies:
            copy.wait()

    vmem = pl.BlockSpec(memory_space=pltpu.VMEM)
    pin = lambda a: pltpu.with_memory_space_constraint(a, pltpu.VMEM)
    return pl.pallas_call(
        kernel,
        out_shape=jax.ShapeDtypeStruct((rows, key_width), jnp.bfloat16),
        in_specs=[pl.BlockSpec(memory_space=pltpu.SMEM)]
        + [vmem] * (2 + pieces)
        + [vmem] * len(arrays),
        out_specs=pl.BlockSpec(memory_space=pl.ANY),
        scratch_shapes=[
            pltpu.VMEM((rank * count, whole), jnp.bfloat16),
            pltpu.VMEM((parts, rows, wide), jnp.bfloat16),
            pltpu.SemaphoreType.DMA((parts,)),
        ],
        compiler_params=pltpu.CompilerParams(vmem_limit_bytes=24 << 20),
        cost_estimate=pl.CostEstimate(
            flops=2 * rows * width * rank * count,
            bytes_accessed=2 * whole * rank * count,
            transcendentals=0,
        ),
        name="shrink_expand",
    )(choice, pin(tokens), pin(mask), *map(pin, bases), *map(pin, arrays))


def join_kernel(shrink, expand, out, arrived):
    width = shrink.shape[2]
    copies = [
        pltpu.make_async_copy(shrink, out.at[:, :, pl.ds(0, width)], arrived.at[0]),
        pltpu.make_async_copy(expand, out.at[:, :, pl.ds(width, expand.shape[2])], arrived.at[1]),
    ]
    for copy in copies:
        copy.start()
    for copy in copies:
        copy.wait()


def joined(shrink, expand):
    held, rank, width = shrink.shape
    pin = lambda a: pltpu.with_memory_space_constraint(a, pltpu.HBM)
    return pl.pallas_call(
        join_kernel,
        out_shape=jax.ShapeDtypeStruct((held, rank, width + expand.shape[2]), shrink.dtype),
        in_specs=[pl.BlockSpec(memory_space=pl.ANY)] * 2,
        out_specs=pl.BlockSpec(memory_space=pltpu.VMEM),
        scratch_shapes=[pltpu.SemaphoreType.DMA((2,))],
        compiler_params=pltpu.CompilerParams(vmem_limit_bytes=8 << 20),
        name="join",
    )(pin(shrink), pin(expand))


def listed(entries):
    arrays, places = [], []
    for array, row in entries:
        known = [array is other for other in arrays]
        if True not in known:
            arrays.append(array)
            known.append(True)
        places.append((known.index(True), row))
    return arrays, places


def picked(choice, ids, batches):
    arrays, places = listed([entry for i in ids for entry in batches[i]])
    _, rank, whole = arrays[0].shape
    last = choice.shape[0] - 1
    held = 2

    def kernel(choice, *refs):
        out, n = refs[-1], 0
        for place, i in enumerate(ids):
            for k in range(len(batches[i])):
                want = choice[i] == k % held
                if len(batches[i]) > held:
                    want = want & (choice[last] == k // held)
                array, row = places[n]
                n += 1

                @pl.when(want)
                def _(place=place, array=array, row=row):
                    out[place] = refs[array][row]

    vmem = pl.BlockSpec(memory_space=pltpu.VMEM)
    return pl.pallas_call(
        kernel,
        out_shape=jax.ShapeDtypeStruct((len(ids), rank, whole), arrays[0].dtype),
        in_specs=[pl.BlockSpec(memory_space=pltpu.SMEM)] + [vmem] * len(arrays),
        out_specs=vmem,
        compiler_params=pltpu.CompilerParams(vmem_limit_bytes=16 << 20),
        name="pick" + "_".join(map(str, ids)),
    )(choice, *(pltpu.with_memory_space_constraint(a, pltpu.VMEM) for a in arrays))


def gridded(tokens, base_weight, shrink_factors, expand_factors, home_rows, requests, block_slot):
    held, rank, width = shrink_factors.shape
    rows_here = tokens.shape[0]
    me = lax.axis_index("store")
    z, y, c = me // 4, me // 2 % 2, me % 2
    inner = (z == 1) | (z == 2)

    def along_z(moves):
        return [(4 * a + r, 4 * b + r) for a, b in moves for r in range(4)]

    def along_y(levels):
        return [(4 * a + r, 4 * a + (r ^ 2)) for a in levels for r in range(4)]

    cores = [(i, i ^ 1) for i in range(16)]
    pairs = along_z([(0, 1), (1, 0), (2, 3), (3, 2)])
    middle = along_z([(1, 2), (2, 1)])
    outward = along_z([(1, 0), (2, 3)])
    every, outer_y = along_y(range(4)), along_y([0, 3])
    send = lambda a, p: lax.ppermute(a, "store", p)
    together = lax.optimization_barrier

    own = joined(shrink_factors, expand_factors)
    p1, y0, p2 = send(own, pairs), send(own, every), send(own, middle)

    wide = expand_factors.shape[2] // 2
    base0 = base_part(tokens, base_weight, 0, wide, requests)
    p1, p2, y0, base0, home_rows, requests, block_slot = together(
        (p1, p2, y0, base0, home_rows, requests, block_slot)
    )
    either = lambda a, b: jnp.where(inner, a, b)
    for_m1, for_n1, for_p3 = together((either(p2, y0), either(p2, p1), p1))
    m1, n1, p3 = send(for_m1, pairs), send(for_n1, every), send(for_p3, middle)

    adapters = jnp.arange(home_rows.shape[0], dtype=jnp.int32)
    stored = jnp.sum(
        jnp.where(requests[0][:, None] == adapters[None, :], home_rows[None, :], 0), axis=1
    )
    stored_other = send(stored, cores)
    second = jnp.where(z < 2, 2, 1)
    third = jnp.where(z < 2, 3, 0)
    chip = lambda level, side: 2 * level + side
    chips = jnp.stack(
        [
            chip(z, y), chip(z ^ 1, y), chip(z, y ^ 1), chip(z ^ 1, y ^ 1),
            chip(second, y), chip(third, y), chip(second, y ^ 1), chip(third, y ^ 1),
        ]
    )
    here = (2 * chips + c).astype(jnp.int32)
    source = jnp.concatenate([here, (2 * chips + 1 - c).astype(jnp.int32)])
    hit = source[:, None] == (stored // held)[None, :]
    slots = jnp.arange(requests.shape[1], dtype=jnp.int32)
    column_slot = jnp.max(jnp.where(hit, slots[None, :], -1), axis=1)
    column_slot = jnp.broadcast_to(column_slot[:, None], (source.shape[0], rank)).reshape(-1)
    row_slot = jnp.broadcast_to(block_slot[0][:, None], (block_slot.shape[1], 16)).reshape(rows_here)
    mask = (row_slot[:, None] == column_slot[None, :]).astype(jnp.bfloat16)

    def second_wanted(rows):
        return jnp.max(
            jnp.where(here[:, None] == (rows // held)[None, :], (rows % held)[None, :], 0), axis=1
        )

    level = inner.astype(jnp.int32)[None]
    take_mine = jnp.concatenate([second_wanted(stored), level])
    take_other = jnp.concatenate([second_wanted(stored_other), level])

    after = lambda a: together((requests, a))[0]
    base1 = base_part(tokens, base_weight, wide, wide, after(p1))
    m1, n1, p3, base1, mask, take_mine, take_other = together(
        (m1, n1, p3, base1, mask, take_mine, take_other)
    )
    batches = [
        [(own, 0), (own, 1)],
        [(p1, 0), (p1, 1)],
        [(y0, 0), (y0, 1)],
        [(n1, 0), (n1, 1), (m1, 0), (m1, 1)],
        [(m1, 0), (m1, 1), (p2, 0), (p2, 1)],
    ]
    p5a, p5b = send(p3[:1], outward), send(p3[1:], outward)
    for_n2, first = together((either(p3, m1), picked(take_other, range(5), batches)))
    n2b, n2a = send(for_n2[1:], every), send(for_n2[:1], every)
    y5, w5 = send(p5a, outer_y), send(n2b, outward)
    batches += [
        [(p5a, 0), (p5b, 0), (p3, 0), (p3, 1)],
        [(n2a, 0), (n2b, 0), (n1, 0), (n1, 1)],
        [(y5, 0), (w5, 0), (n2a, 0), (n2b, 0)],
    ]
    picks = [first] + [picked(take_other, ids, batches) for ids in ((5, 6), (7,))]
    sent = [send(a, cores) for a in picks]
    given = [(a, row) for a in sent for row in range(a.shape[0])]
    return finish(take_mine, tokens, mask, [base0, base1], batches, given)


def solution(mesh):
    placed = (
        P(("groups", "store"), "tensor"),
        P("tensor", None),
        P(("groups", "store"), None, "tensor"),
        P(("groups", "store"), None, None),
        P("groups"),
        P(("groups", "store"), None),
        P(("groups", "store"), None),
    )
    by_grid = mesh.shape["tensor"] == 1 and mesh.shape["store"] == 16
    return jax.shard_map(
        gridded if by_grid else general,
        mesh=mesh,
        in_specs=placed,
        out_specs=P(("groups", "store", "tensor"), None),
        check_vma=False,
    )
```

```python
import functools

import jax
import jax.numpy as jnp
from jax import lax
from jax.experimental import pallas as pl
from jax.experimental.pallas import tpu as pltpu
from jax.sharding import PartitionSpec as P


def general(tokens, base_weight, shrink_factors, expand_factors, home_rows, requests, block_slot):
    slot_count = requests.shape[1]
    rank = shrink_factors.shape[1]
    width = shrink_factors.shape[2]
    rows_here = tokens.shape[0]
    wanted = requests[0]
    adapters = jnp.arange(home_rows.shape[0], dtype=jnp.int32)
    stored = jnp.sum(jnp.where(wanted[:, None] == adapters[None, :], home_rows[None, :], 0), axis=1)
    both = jnp.concatenate([shrink_factors, expand_factors], axis=2)
    everyone = lax.all_gather(both, "store", axis=0, tiled=True)
    picked = jnp.concatenate(
        [lax.dynamic_slice_in_dim(everyone, stored[s], 1, 0) for s in range(slot_count)], axis=0
    ).reshape(slot_count * rank, -1)
    slot_of_row = jnp.broadcast_to(block_slot[0][:, None], (block_slot.shape[1], 16)).reshape(rows_here)
    column_slot = jnp.arange(slot_count * rank, dtype=jnp.int32) // rank
    mask = (slot_of_row[:, None] == column_slot[None, :]).astype(jnp.float32)
    shrink = lax.dot_general(
        tokens, picked[:, :width], (((1,), (1,)), ((), ())), preferred_element_type=jnp.float32
    )
    shrink = lax.psum_scatter(shrink * mask, "tensor", scatter_dimension=0, tiled=True)
    base = lax.psum_scatter(
        jnp.dot(tokens, base_weight, preferred_element_type=jnp.float32),
        "tensor",
        scatter_dimension=0,
        tiled=True,
    )
    expand = jnp.dot(shrink, picked[:, width:].astype(jnp.float32), precision=lax.Precision.HIGHEST)
    return (base + expand).astype(jnp.bfloat16)


def base_part(tokens, weight, start, wide, after):
    rows, width = tokens.shape
    chunks = 8
    depth = width // chunks

    def kernel(after, tokens, weight, out, kept, held, arrived):
        copies = []
        for k in range(chunks):
            span = pl.ds(depth * k, depth)
            for source, target, kind in (
                (weight.at[span, pl.ds(start, wide)], held.at[span, :], 0),
                (tokens.at[:, span], kept.at[:, span], 1),
            ):
                copies.append(pltpu.make_async_copy(source, target, arrived.at[kind, k]))
        for copy in copies:
            copy.start()
        for k in range(chunks):
            for copy in copies[2 * k : 2 * k + 2]:
                copy.wait()
            span = pl.ds(depth * k, depth)
            term = jnp.dot(kept[:, span], held[span, :], preferred_element_type=jnp.float32)
            if k == 0:
                out[...] = term
            else:
                out[...] += term

    anywhere = pl.BlockSpec(memory_space=pl.ANY)
    return pl.pallas_call(
        kernel,
        out_shape=jax.ShapeDtypeStruct((rows, wide), jnp.float32),
        in_specs=[anywhere] * 3,
        out_specs=pl.BlockSpec(memory_space=pltpu.VMEM),
        scratch_shapes=[
            pltpu.VMEM((rows, width), tokens.dtype),
            pltpu.VMEM((width, wide), weight.dtype),
            pltpu.SemaphoreType.DMA((2, chunks)),
        ],
        compiler_params=pltpu.CompilerParams(vmem_limit_bytes=32 << 20),
        cost_estimate=pl.CostEstimate(
            flops=2 * rows * width * wide, bytes_accessed=2 * width * wide, transcendentals=0
        ),
        name=f"base{start}",
    )(*(pltpu.with_memory_space_constraint(a, pltpu.HBM) for a in (after, tokens, weight)))


def finish(choice, tokens, mask, bases, batches, given):
    rows, width = tokens.shape
    _, rank, whole = batches[0][0][0].shape
    key_width = whole - width
    count = len(batches) + len(given)
    last = choice.shape[0] - 1
    pieces = len(bases)
    entries = [entry for batch in batches for entry in batch] + given
    arrays, spots = listed(entries)
    parts = 2 * pieces
    wide = key_width // parts
    owners = [(i, k, len(batch) > 2) for i, batch in enumerate(batches) for k in range(len(batch))]
    owners += [(len(batches) + i, None, False) for i in range(len(given))]
    places = [(i, buf, row, k, levels) for (i, k, levels), (buf, row) in zip(owners, spots)]

    def kernel(choice, tokens, mask, *rest):
        base_refs, bufs = rest[:pieces], rest[pieces:-4]
        out, table, done, left = rest[-4:]
        for i, buf, row, k, levels in places:
            at = pl.ds(rank * i, rank)
            if k is None:
                table[at, :] = bufs[buf][row]
                continue
            want = choice[i] == k % 2
            if levels:
                want = want & (choice[last] == k // 2)

            @pl.when(want)
            def _(at=at, buf=buf, row=row):
                table[at, :] = bufs[buf][row]

        shrink = lax.dot_general(
            tokens[...],
            table[:, :width],
            (((1,), (1,)), ((), ())),
            preferred_element_type=jnp.float32,
        )
        shrink = shrink * mask[...].astype(jnp.float32)
        high = shrink.astype(jnp.bfloat16)
        low = (shrink - high.astype(jnp.float32)).astype(jnp.bfloat16)
        copies = []
        for i in range(parts):
            start = wide * i
            each = parts // pieces
            base = base_refs[i // each][:, pl.ds(wide * (i % each), wide)]
            cols = pl.ds(width + start, wide)
            part = jnp.dot(high, table[:, cols], preferred_element_type=jnp.float32)
            part += jnp.dot(low, table[:, cols], preferred_element_type=jnp.float32)
            done[i] = (base + part).astype(out.dtype)
            copies.append(
                pltpu.make_async_copy(done.at[i], out.at[:, pl.ds(start, wide)], left.at[i])
            )
            copies[-1].start()
        for copy in copies:
            copy.wait()

    vmem = pl.BlockSpec(memory_space=pltpu.VMEM)
    pin = lambda a: pltpu.with_memory_space_constraint(a, pltpu.VMEM)
    return pl.pallas_call(
        kernel,
        out_shape=jax.ShapeDtypeStruct((rows, key_width), jnp.bfloat16),
        in_specs=[pl.BlockSpec(memory_space=pltpu.SMEM)]
        + [vmem] * (2 + pieces)
        + [vmem] * len(arrays),
        out_specs=pl.BlockSpec(memory_space=pl.ANY),
        scratch_shapes=[
            pltpu.VMEM((rank * count, whole), jnp.bfloat16),
            pltpu.VMEM((parts, rows, wide), jnp.bfloat16),
            pltpu.SemaphoreType.DMA((parts,)),
        ],
        compiler_params=pltpu.CompilerParams(vmem_limit_bytes=24 << 20),
        cost_estimate=pl.CostEstimate(
            flops=2 * rows * width * rank * count,
            bytes_accessed=2 * whole * rank * count,
            transcendentals=0,
        ),
        name="shrink_expand",
    )(choice, pin(tokens), pin(mask), *map(pin, bases), *map(pin, arrays))


def join_kernel(shrink, expand, out, arrived):
    width = shrink.shape[2]
    copies = [
        pltpu.make_async_copy(shrink, out.at[:, :, pl.ds(0, width)], arrived.at[0]),
        pltpu.make_async_copy(expand, out.at[:, :, pl.ds(width, expand.shape[2])], arrived.at[1]),
    ]
    for copy in copies:
        copy.start()
    for copy in copies:
        copy.wait()


def joined(shrink, expand):
    held, rank, width = shrink.shape
    pin = lambda a: pltpu.with_memory_space_constraint(a, pltpu.HBM)
    return pl.pallas_call(
        join_kernel,
        out_shape=jax.ShapeDtypeStruct((held, rank, width + expand.shape[2]), shrink.dtype),
        in_specs=[pl.BlockSpec(memory_space=pl.ANY)] * 2,
        out_specs=pl.BlockSpec(memory_space=pltpu.VMEM),
        scratch_shapes=[pltpu.SemaphoreType.DMA((2,))],
        compiler_params=pltpu.CompilerParams(vmem_limit_bytes=8 << 20),
        name="join",
    )(pin(shrink), pin(expand))


def listed(entries):
    arrays, places = [], []
    for array, row in entries:
        known = [array is other for other in arrays]
        if True not in known:
            arrays.append(array)
            known.append(True)
        places.append((known.index(True), row))
    return arrays, places


def picked(choice, ids, batches):
    arrays, places = listed([entry for i in ids for entry in batches[i]])
    _, rank, whole = arrays[0].shape
    last = choice.shape[0] - 1
    held = 2

    def kernel(choice, *refs):
        out, n = refs[-1], 0
        for place, i in enumerate(ids):
            for k in range(len(batches[i])):
                want = choice[i] == k % held
                if len(batches[i]) > held:
                    want = want & (choice[last] == k // held)
                array, row = places[n]
                n += 1

                @pl.when(want)
                def _(place=place, array=array, row=row):
                    out[place] = refs[array][row]

    vmem = pl.BlockSpec(memory_space=pltpu.VMEM)
    return pl.pallas_call(
        kernel,
        out_shape=jax.ShapeDtypeStruct((len(ids), rank, whole), arrays[0].dtype),
        in_specs=[pl.BlockSpec(memory_space=pltpu.SMEM)] + [vmem] * len(arrays),
        out_specs=vmem,
        compiler_params=pltpu.CompilerParams(vmem_limit_bytes=16 << 20),
        name="pick" + "_".join(map(str, ids)),
    )(choice, *(pltpu.with_memory_space_constraint(a, pltpu.VMEM) for a in arrays))


def gridded(tokens, base_weight, shrink_factors, expand_factors, home_rows, requests, block_slot):
    held, rank, width = shrink_factors.shape
    rows_here = tokens.shape[0]
    me = lax.axis_index("store")
    z, y, c = me // 4, me // 2 % 2, me % 2
    inner = (z == 1) | (z == 2)

    def along_z(moves):
        return [(4 * a + r, 4 * b + r) for a, b in moves for r in range(4)]

    def along_y(levels):
        return [(4 * a + r, 4 * a + (r ^ 2)) for a in levels for r in range(4)]

    cores = [(i, i ^ 1) for i in range(16)]
    pairs = along_z([(0, 1), (1, 0), (2, 3), (3, 2)])
    middle = along_z([(1, 2), (2, 1)])
    outward = along_z([(1, 0), (2, 3)])
    every, outer_y = along_y(range(4)), along_y([0, 3])
    send = lambda a, p: lax.ppermute(a, "store", p)
    together = lax.optimization_barrier

    own = joined(shrink_factors, expand_factors)
    p1, y0, p2 = send(own, pairs), send(own, every), send(own, middle)

    wide = expand_factors.shape[2] // 2
    base0 = base_part(tokens, base_weight, 0, wide, requests)
    p1, p2, y0, base0, home_rows, requests, block_slot = together(
        (p1, p2, y0, base0, home_rows, requests, block_slot)
    )
    either = lambda a, b: jnp.where(inner, a, b)
    for_m1, for_n1, for_p3 = together((either(p2, y0), either(p2, p1), p1))
    m1, n1, p3 = send(for_m1, pairs), send(for_n1, every), send(for_p3, middle)

    adapters = jnp.arange(home_rows.shape[0], dtype=jnp.int32)
    stored = jnp.sum(
        jnp.where(requests[0][:, None] == adapters[None, :], home_rows[None, :], 0), axis=1
    )
    stored_other = send(stored, cores)
    second = jnp.where(z < 2, 2, 1)
    third = jnp.where(z < 2, 3, 0)
    chip = lambda level, side: 2 * level + side
    chips = jnp.stack(
        [
            chip(z, y), chip(z ^ 1, y), chip(z, y ^ 1), chip(z ^ 1, y ^ 1),
            chip(second, y), chip(third, y), chip(second, y ^ 1), chip(third, y ^ 1),
        ]
    )
    here = (2 * chips + c).astype(jnp.int32)
    source = jnp.concatenate([here, (2 * chips + 1 - c).astype(jnp.int32)])
    hit = source[:, None] == (stored // held)[None, :]
    slots = jnp.arange(requests.shape[1], dtype=jnp.int32)
    column_slot = jnp.max(jnp.where(hit, slots[None, :], -1), axis=1)
    column_slot = jnp.broadcast_to(column_slot[:, None], (source.shape[0], rank)).reshape(-1)
    row_slot = jnp.broadcast_to(block_slot[0][:, None], (block_slot.shape[1], 16)).reshape(rows_here)
    mask = (row_slot[:, None] == column_slot[None, :]).astype(jnp.bfloat16)

    def second_wanted(rows):
        return jnp.max(
            jnp.where(here[:, None] == (rows // held)[None, :], (rows % held)[None, :], 0), axis=1
        )

    level = inner.astype(jnp.int32)[None]
    take_mine = jnp.concatenate([second_wanted(stored), level])
    take_other = jnp.concatenate([second_wanted(stored_other), level])

    after = lambda a: together((requests, a))[0]
    base1 = base_part(tokens, base_weight, wide, wide, after(p1))
    m1, n1, p3, base1, mask, take_mine, take_other = together(
        (m1, n1, p3, base1, mask, take_mine, take_other)
    )
    batches = [
        [(own, 0), (own, 1)],
        [(p1, 0), (p1, 1)],
        [(y0, 0), (y0, 1)],
        [(n1, 0), (n1, 1), (m1, 0), (m1, 1)],
        [(m1, 0), (m1, 1), (p2, 0), (p2, 1)],
    ]
    p5a, p5b = send(p3[:1], outward), send(p3[1:], outward)
    for_n2, first = together((either(p3, m1), picked(take_other, range(5), batches)))
    n2b, n2a = send(for_n2[1:], every), send(for_n2[:1], every)
    y5, w5 = send(p5a, outer_y), send(n2b, outward)
    batches += [
        [(p5a, 0), (p5b, 0), (p3, 0), (p3, 1)],
        [(n2a, 0), (n2b, 0), (n1, 0), (n1, 1)],
        [(y5, 0), (w5, 0), (n2a, 0), (n2b, 0)],
    ]
    picks = [first] + [picked(take_other, ids, batches) for ids in ((5, 6), (7,))]
    sent = [send(a, cores) for a in picks]
    given = [(a, row) for a in sent for row in range(a.shape[0])]
    return finish(take_mine, tokens, mask, [base0, base1], batches, given)


def solution(mesh):
    placed = (
        P(("groups", "store"), "tensor"),
        P("tensor", None),
        P(("groups", "store"), None, "tensor"),
        P(("groups", "store"), None, None),
        P("groups"),
        P(("groups", "store"), None),
        P(("groups", "store"), None),
    )
    by_grid = mesh.shape["tensor"] == 1 and mesh.shape["store"] == 16
    return jax.shard_map(
        gridded if by_grid else general,
        mesh=mesh,
        in_specs=placed,
        out_specs=P(("groups", "store", "tensor"), None),
        check_vma=False,
    )
```
